32 devices in a mesh: dp: 8 (over z, x), section: 2 (over core), tensor: 2 (over y).
Axes of the slice: x: 2, y: 2, z: 4, core: 2. Of those that a mesh axis runs over, the one named last changes fastest.
Arguments:
- source_tokens: bfloat16 [4096, 4096], P('dp'), may hold values from -6 to 6
- destination: int32 [4096], P('dp'), may hold values from -1 to 7, as said below
- segment_ids: int32 [4096], P('dp'), may hold values from -1 to 4095, as said below
- positions: int32 [4096], P('dp'), may hold values from 0 to 63, as said below
- norm_gain: float32 [2, 4096], P('section'), may hold values from 0.1 to 1.9
- w_query: bfloat16 [2, 4096, 4096], P('section', 'dp', 'tensor')
- w_key: bfloat16 [2, 4096, 1024], P('section', 'dp', 'tensor')
- w_value: bfloat16 [2, 4096, 1024], P('section', 'dp', 'tensor'), may hold values from -0.09375 to 0.09375
- w_out: bfloat16 [2, 4096, 4096], P('section', 'tensor', 'dp'), may hold values from -0.09375 to 0.09375
Outputs:
- final_states: bfloat16 [4096, 4096], P(('dp', 'section', 'tensor'))
The draws below stay inside these ranges and needn't reach their ends.
Inputs may be any that keep to these rules, and one draw needn't show every extreme that they name: `destination`: -1 marks an empty source row, otherwise the receiving replica. A device's rows that name one replica stand together in order and hold whole sequences; at most 64 of a device's rows name one replica, and in every draw one replica receives exactly 64 from every device. `segment_ids`: equal for the tokens of one sequence and different between sequences anywhere; -1 on empty rows. `positions`: 0 at a sequence's first token and rising by one along it; 0 on empty rows.
All inputs are finite; a program needn't handle non-finite values.
Results may differ from the reference program's by a relative error of at most 0.015.
Values may be sent and summed in bfloat16 or wider, within the bound.
A program may use at most 192 MiB of HBM per device.

```python
import jax
import jax.numpy as jnp
from jax import lax

D = 4096
HEADS = 32
KV_HEADS = 8
HEAD_DIM = 128
PACK = 512
ROWS = 256
SOURCE = 4096
N_DP = 8
N_SECTION = 2
N_TENSOR = 2


def packing(key):
    key = jax.random.fold_in(key, 101)
    key_count, key_full, key_order, key_break = jax.random.split(key, 4)
    capacity = PACK // N_DP
    senders = jnp.arange(N_DP, dtype=jnp.int32)
    counts = jax.random.randint(key_count, (N_DP, N_DP), 1, capacity + 1)
    fullest = jax.random.randint(key_full, (), 0, N_DP)
    counts = jnp.where(senders[None, :] == fullest, capacity, counts)
    scores = jax.random.randint(key_order, (N_DP, N_DP), 0, 1024) * N_DP + senders[None, :]
    visit_order = jnp.argsort(scores, axis=1).astype(jnp.int32)
    ordered = jnp.take_along_axis(counts, visit_order, axis=1)
    block_ends = jnp.cumsum(ordered, axis=1).astype(jnp.int32)
    starts = block_ends - ordered
    places = jnp.arange(PACK, dtype=jnp.int32)
    inside = (places[None, None, :] >= starts[:, :, None]) & (places[None, None, :] < block_ends[:, :, None])
    block_index = jnp.sum(inside.astype(jnp.int32) * senders[None, :, None], axis=1).astype(jnp.int32)
    occupied = jnp.any(inside, axis=1)
    receiver = jnp.take_along_axis(visit_order, block_index, axis=1)
    offset = places[None, :] - jnp.take_along_axis(starts, block_index, axis=1)
    breaks = jax.random.randint(key_break, (N_DP, PACK), 0, 3) == 0
    single = (senders[:, None] == 0) & (receiver == fullest)
    breaks = breaks & jnp.logical_not(single) | (offset == 0)
    firsts = lax.cummax(jnp.where(breaks, places[None, :], 0), axis=1)
    destination = jnp.where(occupied, receiver, -1)
    segment = jnp.where(occupied, senders[:, None] * PACK + (PACK - 1 - firsts), -1)
    position = jnp.where(occupied, places[None, :] - firsts, 0)
    return (destination.reshape(-1), segment.reshape(-1), position.reshape(-1))


def draw_destination(key, part):
    layout = packing(key)
    return layout[0]


def draw_segment_ids(key, part):
    layout = packing(key)
    return layout[1]


def draw_positions(key, part):
    layout = packing(key)
    return layout[2]


def draw_w_key(key, part):
    key = jax.random.fold_in(key, 4)
    independent = jax.random.normal(key, (N_SECTION, D, KV_HEADS * HEAD_DIM), jnp.float32) * D ** (-0.5)
    return independent.astype(jnp.bfloat16)


def draw_w_query(key, part):
    key = jax.random.fold_in(key, 5)
    independent = jax.random.normal(key, (N_SECTION, D, HEADS * HEAD_DIM), jnp.float32) * D ** (-0.5)
    return independent.astype(jnp.bfloat16)


def block_levels(key, extent, shards, least, top_value):
    level, own = 1.0, jax.random.fold_in(key, 6)
    for dim, shards_of in shards:
        steps = jnp.exp(jax.random.uniform(jax.random.fold_in(own, dim), (shards_of,), jnp.float32, least / len(shards), top_value / len(shards)))
        level = level * jnp.repeat(steps, extent[dim] // shards_of).reshape([-1 if axis == dim else 1 for axis in range(len(extent))])
    return level


def normal_values(own_key, extent, width, limit, cuts=(), kind=jnp.bfloat16):
    level = block_levels(own_key, extent, cuts, -0.22, 0.18) if cuts else 1.0
    drawn = jax.random.normal(own_key, extent, jnp.float32) * width * level
    return jnp.minimum(jnp.maximum(drawn, -limit), limit).astype(kind)


def setup_inputs(seed: int = 0) -> dict:
    seeds = jax.random.split(jax.random.key(seed), 10)
    return {
        "source_tokens": normal_values(seeds[0], (SOURCE, D), 1.0, 6.0, ((0, 8),)),
        "destination": draw_destination(jax.random.fold_in(seeds[9], 71), 0),
        "segment_ids": draw_segment_ids(jax.random.fold_in(seeds[9], 71), 0),
        "positions": draw_positions(jax.random.fold_in(seeds[9], 71), 0),
        "norm_gain": jnp.clip(1.0 + 0.18 * jax.random.normal(seeds[4], (N_SECTION, D), jnp.float32), 0.1, 1.9),
        "w_query": draw_w_query(jax.random.fold_in(seeds[9], 71), 0),
        "w_key": draw_w_key(jax.random.fold_in(seeds[9], 71), 0),
        "w_value": normal_values(seeds[7], (N_SECTION, D, KV_HEADS * HEAD_DIM), D ** -0.5, 0.09375, ((0, 2), (1, 8), (2, 2))),
        "w_out": normal_values(seeds[8], (N_SECTION, HEADS * HEAD_DIM, D), (HEADS * HEAD_DIM) ** -0.5, 0.09375, ((0, 2), (1, 2), (2, 8))),
    }


THETA = 500000.0
EPSILON = 1e-05

def rotate(values, places):
    half_dim = HEAD_DIM // 2
    frequency = THETA ** (-(jnp.arange(half_dim, dtype=jnp.float32) * 2.0) / HEAD_DIM)
    angles = places.astype(jnp.float32)[..., None] * frequency
    cosine = jnp.concatenate([jnp.cos(angles), jnp.cos(angles)], axis=-1)[..., None, :]
    sine_part = jnp.concatenate([jnp.sin(angles), jnp.sin(angles)], axis=-1)[..., None, :]
    turned = jnp.concatenate([-values[..., half_dim:], values[..., :half_dim]], axis=-1)
    return values * cosine + turned * sine_part

def normalize(residual, gain_row):
    widened = residual.astype(jnp.float32)
    inv_scale = lax.rsqrt(lax.optimization_barrier(jnp.mean(widened * widened, axis=-1, keepdims=True)) + EPSILON)
    return (widened * inv_scale * gain_row).astype(jnp.bfloat16)

def attend(normed, w_query, w_key, w_value, id_rows, pos_rows):
    batch_count, row_len = id_rows.shape
    flat_rows = normed.reshape(batch_count * row_len, -1)
    q_heads = w_query.shape[1] // HEAD_DIM
    kv_heads = w_key.shape[1] // HEAD_DIM
    group_size = q_heads // kv_heads
    queries = jnp.dot(flat_rows, w_query, preferred_element_type=jnp.float32)
    key_proj = jnp.dot(flat_rows, w_key, preferred_element_type=jnp.float32)
    value_rows = jnp.dot(flat_rows, w_value, preferred_element_type=jnp.float32).astype(jnp.bfloat16)
    queries = rotate(queries.reshape(batch_count, row_len, q_heads, HEAD_DIM), pos_rows).astype(jnp.bfloat16)
    queries = queries.reshape(batch_count, row_len, kv_heads, group_size, HEAD_DIM)
    key_rows = rotate(key_proj.reshape(batch_count, row_len, kv_heads, HEAD_DIM), pos_rows).astype(jnp.bfloat16)
    value_rows = value_rows.reshape(batch_count, row_len, kv_heads, HEAD_DIM)
    scores = jnp.einsum('brkgd,bskd->bkgrs', queries.astype(jnp.float32), key_rows.astype(jnp.float32)) * HEAD_DIM ** (-0.5)
    allowed = (id_rows[:, :, None] == id_rows[:, None, :]) & (pos_rows[:, None, :] <= pos_rows[:, :, None])
    allowed = allowed[:, None, None]
    scores = jnp.where(allowed, scores, -1e+30)
    row_top = lax.optimization_barrier(jnp.max(scores, axis=-1, keepdims=True))
    powers = jnp.where(allowed, jnp.exp(scores - row_top), 0.0)
    weights = (powers / lax.optimization_barrier(jnp.sum(powers, axis=-1, keepdims=True))).astype(jnp.bfloat16)
    mixed_heads = jnp.einsum('bkgrs,bskd->brkgd', weights.astype(jnp.float32), value_rows.astype(jnp.float32))
    return mixed_heads.astype(jnp.bfloat16).reshape(batch_count * row_len, q_heads * HEAD_DIM)

def layer(residual, gain_row, w_query, w_key, w_value, w_out, id_rows, pos_rows):
    batch_count, row_len = id_rows.shape
    normed = normalize(residual, gain_row)
    mixed_heads = attend(normed, w_query, w_key, w_value, id_rows, pos_rows)
    group_width = w_out.shape[0] // N_TENSOR
    head_total = jnp.zeros((batch_count * row_len, w_out.shape[1]), jnp.float32)
    for member in range(N_TENSOR):
        partial_term = jnp.dot(mixed_heads[:, member * group_width:(member + 1) * group_width], w_out[member * group_width:(member + 1) * group_width], preferred_element_type=jnp.float32).astype(jnp.bfloat16)
        partial_term = lax.optimization_barrier(partial_term)
        head_total = head_total + partial_term.astype(jnp.float32)
    return (residual.astype(jnp.float32) + head_total.reshape(batch_count, row_len, -1)).astype(jnp.bfloat16)

def reference(source_tokens, destination, segment_ids, positions, norm_gain, w_query, w_key, w_value, w_out):
    capacity = PACK // N_DP
    owners = destination.reshape(N_DP, PACK)
    matches = (owners[:, :, None] == jnp.arange(N_DP, dtype=jnp.int32)[None, None, :]).astype(jnp.int32)
    ranking = lax.optimization_barrier(jnp.sum((jnp.cumsum(matches, axis=1) - matches) * matches, axis=2)).astype(jnp.int32)
    sender = jnp.arange(N_DP, dtype=jnp.int32)[:, None]
    targets = jnp.where(owners >= 0, owners * PACK + sender * capacity + ranking, N_DP * PACK)
    targets = targets.reshape(-1).astype(jnp.int32)
    packed = jnp.zeros((N_DP * PACK + 1, D), jnp.bfloat16).at[targets].set(source_tokens)[:-1]
    packed_ids = jnp.full((N_DP * PACK + 1,), -1, jnp.int32).at[targets].set(segment_ids)[:-1]
    packed_pos = jnp.zeros((N_DP * PACK + 1,), jnp.int32).at[targets].set(positions)[:-1]
    residual = packed.reshape(N_DP * N_SECTION, ROWS, D)
    segment_rows = packed_ids.reshape(N_DP * N_SECTION, ROWS)
    position_rows = packed_pos.reshape(N_DP * N_SECTION, ROWS)
    for level in range(N_SECTION):
        residual = layer(residual, norm_gain[level], w_query[level], w_key[level], w_value[level], w_out[level], segment_rows, position_rows)
    return residual.reshape(N_DP * PACK, D)
```

```python
import jax
import jax.numpy as jnp
from jax import lax
from jax.sharding import PartitionSpec as P

HEAD_DIM = 128


THETA = 500000.0
EPSILON = 1e-05
BF16 = jnp.bfloat16
F32 = jnp.float32


def swapped(array, axis):
    return lax.ppermute(array, axis, [(0, 1), (1, 0)])


def join(array, axis, dim):
    if lax.axis_size(axis) != 2:
        return lax.all_gather(array, axis, axis=dim, tiled=True)
    other = swapped(array, axis)
    first = lax.axis_index(axis) == 0
    return jnp.concatenate(
        [jnp.where(first, array, other), jnp.where(first, other, array)], axis=dim
    )


def sum_share(array, axis):
    if lax.axis_size(axis) != 2:
        return lax.psum_scatter(
            array.astype(BF16), axis, scatter_dimension=0, tiled=True
        ).astype(F32)
    half = array.shape[0] // 2
    first = lax.axis_index(axis) == 0
    mine = jnp.where(first, array[:half], array[half:])
    theirs = jnp.where(first, array[half:], array[:half]).astype(BF16)
    return mine + swapped(theirs, axis).astype(F32)


def both_layers(own, dim, split):
    first = lax.axis_index("section") == 0
    if split:
        half = own.shape[dim] // 2
        low = lax.slice_in_dim(own, 0, half, axis=dim)
        high = lax.slice_in_dim(own, half, 2 * half, axis=dim)
        mine, give = jnp.where(first, low, high), jnp.where(first, high, low)
    else:
        mine = give = own
    got = swapped(give, "section")
    return jnp.where(first, mine, got), jnp.where(first, got, mine)


def ring_order(count):
    return [2 * i for i in range(count // 2)] + [
        2 * i + 1 for i in reversed(range(count // 2))
    ]


def ring_gather(own, before):
    count = lax.axis_size("dp")
    order = ring_order(count)
    right = [(order[i], order[(i + 1) % count]) for i in range(count)]
    left = [(b, a) for a, b in right]
    parts = [None] * count
    parts[0] = own
    onward = back = own
    if before is not None:
        onward, back, _, _ = lax.optimization_barrier((own, own) + before)
    for hop in range(1, count // 2):
        onward = lax.ppermute(onward, "dp", right)
        back = lax.ppermute(back, "dp", left)
        parts[hop], parts[count - hop] = onward, back
    half = own.shape[0] // 2
    top = lax.ppermute(onward[:half], "dp", right)
    low = lax.ppermute(back[half:], "dp", left)
    parts[count // 2] = jnp.concatenate([top, low], axis=0)
    return parts, (onward, back)


def turn_factors(places):
    half_dim = HEAD_DIM // 2
    frequency = THETA ** (-(jnp.arange(half_dim, dtype=F32) * 2.0) / HEAD_DIM)
    angles = places.astype(F32)[..., None] * frequency
    cosine, sine = jnp.cos(angles), jnp.sin(angles)
    return (
        jnp.concatenate([cosine, cosine], axis=-1)[..., None, :],
        jnp.concatenate([sine, sine], axis=-1)[..., None, :],
    )


def rotate(values, factors):
    half_dim = HEAD_DIM // 2
    turned = jnp.concatenate([-values[..., half_dim:], values[..., :half_dim]], axis=-1)
    return values * factors[0] + turned * factors[1]


def attend_local(projected, allowed, factors, query_width, key_width):
    batches, row_len = allowed.shape[:2]
    q_heads = query_width // HEAD_DIM
    kv_heads = key_width // HEAD_DIM
    group_size = q_heads // kv_heads
    projected = projected.reshape(batches, row_len, -1)
    queries = rotate(
        projected[..., :query_width].reshape(batches, row_len, q_heads, HEAD_DIM), factors
    ).astype(BF16)
    queries = queries.reshape(batches, row_len, kv_heads, group_size, HEAD_DIM)
    key_rows = rotate(
        projected[..., query_width : query_width + key_width].reshape(
            batches, row_len, kv_heads, HEAD_DIM
        ),
        factors,
    ).astype(BF16)
    value_rows = (
        projected[..., query_width + key_width :]
        .astype(BF16)
        .reshape(batches, row_len, kv_heads, HEAD_DIM)
    )
    scores = jnp.einsum(
        "brkgd,bskd->bkgrs", queries, key_rows, preferred_element_type=F32
    ) * HEAD_DIM ** (-0.5)
    allowed = allowed[:, None, None]
    scores = jnp.where(allowed, scores, -1e30)
    row_top = jnp.max(scores, axis=-1, keepdims=True)
    powers = jnp.where(allowed, jnp.exp(scores - row_top), 0.0)
    weights = (powers / jnp.sum(powers, axis=-1, keepdims=True)).astype(BF16)
    mixed_heads = jnp.einsum(
        "bkgrs,bskd->brkgd", weights, value_rows, preferred_element_type=F32
    )
    return mixed_heads.astype(BF16).reshape(batches * row_len, query_width)


def per_device(
    source_tokens, destination, segment_ids, positions, norm_gain, w_query, w_key, w_value, w_out
):
    replicas = lax.axis_size("dp")
    phases = lax.axis_size("section")
    tensors = lax.axis_size("tensor")
    section = lax.axis_index("section")
    tensor = lax.axis_index("tensor")
    packed_len, width = source_tokens.shape
    capacity = packed_len // replicas
    row_count = packed_len // phases
    row_share = row_count // tensors
    chunk = width // replicas
    place = lax.axis_index("dp")
    spot = jnp.where(place % 2 == 0, place // 2, replicas - 1 - place // 2)

    def start_of(k):
        there = (spot - k + replicas) % replicas
        owner = jnp.where(there < replicas // 2, 2 * there, 2 * (replicas - 1 - there) + 1)
        return owner * chunk

    split = (w_key.shape[2] // HEAD_DIM) % phases == 0
    query_parts = both_layers(w_query[0], 1, True)
    kv_parts = both_layers(
        jnp.stack([w_key[0], w_value[0]], axis=1), 2, split
    )
    query_width = query_parts[0].shape[1]
    key_width = kv_parts[0].shape[2]
    joined = [
        jnp.concatenate([q, kv.reshape(kv.shape[0], -1)], axis=1)
        for q, kv in zip(query_parts, kv_parts)
    ]
    out_parts = both_layers(w_out[0], 0, True)
    first = section == 0
    other_gain = swapped(norm_gain[0], "section")
    gains = (
        jnp.where(first, norm_gain[0], other_gain),
        jnp.where(first, other_gain, norm_gain[0]),
    )

    matches = destination[:, None] == jnp.arange(replicas, dtype=jnp.int32)[None, :]
    counts = jnp.sum(matches.astype(jnp.int32), axis=0)
    firsts = jnp.min(
        jnp.where(matches, jnp.arange(packed_len, dtype=jnp.int32)[:, None], packed_len), axis=0
    )
    offsets = jnp.arange(capacity, dtype=jnp.int32)
    filled = offsets[None, :] < counts[:, None]
    chosen = jnp.where(filled, firsts[:, None] + offsets[None, :], 0).reshape(-1)
    filled_flat = filled.reshape(-1)
    share = width // (phases * tensors)
    columns = lax.dynamic_slice_in_dim(
        source_tokens, (section * tensors + tensor) * share, share, 1
    )
    send_rows = jnp.where(filled_flat[:, None], columns[chosen], 0).reshape(
        replicas, capacity, share
    )
    send_ids = jnp.where(filled_flat, segment_ids[chosen], -1).reshape(replicas, capacity)
    send_pos = jnp.where(filled_flat, positions[chosen], 0).reshape(replicas, capacity)
    got_rows = lax.all_to_all(send_rows, "dp", split_axis=0, concat_axis=0, tiled=True)
    got_marks = lax.all_to_all(
        jnp.concatenate([send_ids, send_pos], axis=1), "dp", split_axis=0, concat_axis=0, tiled=True
    )
    packed = join(join(got_rows.reshape(packed_len, share), "tensor", 1), "section", 1)
    id_rows = got_marks[:, :capacity].reshape(phases, row_count)
    pos_rows = got_marks[:, capacity:].reshape(phases, row_count)
    factors = turn_factors(pos_rows)
    allowed = (id_rows[:, :, None] == id_rows[:, None, :]) & (
        pos_rows[:, None, :] <= pos_rows[:, :, None]
    )

    starts = [start_of(k) for k in range(replicas)]
    states = [lax.dynamic_slice_in_dim(packed, s, chunk, 1) for s in starts]
    before = None
    for level in range(phases):
        projections, before = ring_gather(joined[level], before)
        outs, before = ring_gather(out_parts[level], before)
        total = sum(
            jnp.sum(jnp.square(piece.astype(F32)), axis=-1, keepdims=True) for piece in states
        )
        inv_scale = lax.rsqrt(total / width + EPSILON)
        projected = 0.0
        for k in range(replicas):
            gain = lax.dynamic_slice_in_dim(gains[level], starts[k], chunk, 0)
            normed = (states[k].astype(F32) * inv_scale * gain).astype(BF16)
            projected += jnp.dot(normed, projections[k], preferred_element_type=F32)
        mixed_heads = attend_local(projected, allowed, factors, query_width, key_width)
        fresh = [None] * replicas
        half = replicas // 2
        rounds = [[0]] + [[k, replicas - k] for k in range(1, half)] + [[half]]
        for members in rounds:
            terms = jnp.concatenate(
                [jnp.dot(mixed_heads, outs[k], preferred_element_type=F32) for k in members],
                axis=1,
            )
            share_sum = sum_share(sum_share(terms, "section"), "tensor")
            held = jnp.concatenate([states[k] for k in members], axis=1)
            held = lax.dynamic_slice_in_dim(
                held, section * row_count + tensor * row_share, row_share, 0
            )
            result = (held.astype(F32) + share_sum).astype(BF16)
            if level < phases - 1:
                result = join(join(result, "tensor", 0), "section", 0)
            for i, k in enumerate(members):
                fresh[k] = lax.slice_in_dim(result, i * chunk, (i + 1) * chunk, axis=1)
        states = fresh
    final = jnp.zeros((row_share, width), BF16)
    for k in range(replicas):
        final = lax.dynamic_update_slice_in_dim(final, states[k], starts[k], 1)
    return final


def solution(mesh):
    return jax.shard_map(
        per_device,
        mesh=mesh,
        in_specs=(
            P("dp", None),
            P("dp"),
            P("dp"),
            P("dp"),
            P("section", None),
            P("section", "dp", "tensor"),
            P("section", "dp", "tensor"),
            P("section", "dp", "tensor"),
            P("section", "tensor", "dp"),
        ),
        out_specs=P(("dp", "section", "tensor"), None),
        check_vma=False,
    )
```

```python
import jax
import jax.numpy as jnp
from jax import lax
from jax.sharding import PartitionSpec as P

HEAD_DIM = 128


THETA = 500000.0
EPSILON = 1e-05
BF16 = jnp.bfloat16
F32 = jnp.float32


def swapped(array, axis):
    return lax.ppermute(array, axis, [(0, 1), (1, 0)])


def join(array, axis, dim):
    if lax.axis_size(axis) != 2:
        return lax.all_gather(array, axis, axis=dim, tiled=True)
    other = swapped(array, axis)
    first = lax.axis_index(axis) == 0
    return jnp.concatenate(
        [jnp.where(first, array, other), jnp.where(first, other, array)], axis=dim
    )


def sum_share(array, axis):
    if lax.axis_size(axis) != 2:
        return lax.psum_scatter(
            array.astype(BF16), axis, scatter_dimension=0, tiled=True
        ).astype(F32)
    half = array.shape[0] // 2
    first = lax.axis_index(axis) == 0
    mine = jnp.where(first, array[:half], array[half:])
    theirs = jnp.where(first, array[half:], array[:half]).astype(BF16)
    return mine + swapped(theirs, axis).astype(F32)


def both_layers(shards, dim, splits):
    section = lax.axis_index("section")
    mine, give = [], []
    for own, split in zip(shards, splits):
        half = own.shape[dim] // 2
        for place, kept in ((section, mine), (1 - section, give)):
            kept.append(
                lax.dynamic_slice_in_dim(own, place * half, half, dim) if split else own
            )
    mine, give = jnp.concatenate(mine, axis=dim), jnp.concatenate(give, axis=dim)
    got = swapped(give, "section")
    return jnp.where(section == 0, mine, got), jnp.where(section == 0, got, mine)


def ring_order(count):
    return [2 * i for i in range(count // 2)] + [
        2 * i + 1 for i in reversed(range(count // 2))
    ]


def ring_gather(own, before):
    count = lax.axis_size("dp")
    order = ring_order(count)
    right = [(order[i], order[(i + 1) % count]) for i in range(count)]
    left = [(b, a) for a, b in right]
    parts = [None] * count
    parts[0] = own
    onward = back = own
    if before is not None:
        onward, back, _, _ = lax.optimization_barrier((own, own) + before)
    for hop in range(1, count // 2):
        onward = lax.ppermute(onward, "dp", right)
        back = lax.ppermute(back, "dp", left)
        parts[hop], parts[count - hop] = onward, back
    half = own.shape[0] // 2
    top = lax.ppermute(onward[:half], "dp", right)
    low = lax.ppermute(back[half:], "dp", left)
    parts[count // 2] = jnp.concatenate([top, low], axis=0)
    return parts, (onward, back)


def turn_factors(places):
    half_dim = HEAD_DIM // 2
    frequency = THETA ** (-(jnp.arange(half_dim, dtype=F32) * 2.0) / HEAD_DIM)
    angles = places.astype(F32)[..., None] * frequency
    cosine, sine = jnp.cos(angles), jnp.sin(angles)
    return (
        jnp.concatenate([cosine, cosine], axis=-1)[..., None, :],
        jnp.concatenate([sine, sine], axis=-1)[..., None, :],
    )


def rotate(values, factors):
    half_dim = HEAD_DIM // 2
    turned = jnp.concatenate([-values[..., half_dim:], values[..., :half_dim]], axis=-1)
    return values * factors[0] + turned * factors[1]


def attend_local(projected, allowed, factors, query_width, key_width):
    batches, row_len = allowed.shape[:2]
    q_heads = query_width // HEAD_DIM
    kv_heads = key_width // HEAD_DIM
    group_size = q_heads // kv_heads
    projected = projected.reshape(batches, row_len, -1)
    queries = rotate(
        projected[..., :query_width].reshape(batches, row_len, q_heads, HEAD_DIM), factors
    ).astype(BF16)
    queries = queries.reshape(batches, row_len, kv_heads, group_size, HEAD_DIM)
    key_rows = rotate(
        projected[..., query_width : query_width + key_width].reshape(
            batches, row_len, kv_heads, HEAD_DIM
        ),
        factors,
    ).astype(BF16)
    value_rows = (
        projected[..., query_width + key_width :]
        .astype(BF16)
        .reshape(batches, row_len, kv_heads, HEAD_DIM)
    )
    scores = jnp.einsum(
        "brkgd,bskd->bkgrs", queries, key_rows, preferred_element_type=F32
    ) * HEAD_DIM ** (-0.5)
    allowed = allowed[:, None, None]
    scores = jnp.where(allowed, scores, -1e30)
    row_top = jnp.max(scores, axis=-1, keepdims=True)
    powers = jnp.where(allowed, jnp.exp(scores - row_top), 0.0)
    weights = (powers / jnp.sum(powers, axis=-1, keepdims=True)).astype(BF16)
    mixed_heads = jnp.einsum(
        "bkgrs,bskd->brkgd", weights, value_rows, preferred_element_type=F32
    )
    return mixed_heads.astype(BF16).reshape(batches * row_len, query_width)


def per_device(
    source_tokens, destination, segment_ids, positions, norm_gain, w_query, w_key, w_value, w_out
):
    replicas = lax.axis_size("dp")
    phases = lax.axis_size("section")
    tensors = lax.axis_size("tensor")
    section = lax.axis_index("section")
    tensor = lax.axis_index("tensor")
    packed_len, width = source_tokens.shape
    capacity = packed_len // replicas
    row_count = packed_len // phases
    row_share = row_count // tensors
    chunk = width // replicas
    place = lax.axis_index("dp")
    spot = jnp.where(place % 2 == 0, place // 2, replicas - 1 - place // 2)

    def start_of(k):
        there = (spot - k + replicas) % replicas
        owner = jnp.where(there < replicas // 2, 2 * there, 2 * (replicas - 1 - there) + 1)
        return owner * chunk

    split = (w_key.shape[2] // HEAD_DIM) % phases == 0
    joined = both_layers((w_query[0], w_key[0], w_value[0]), 1, (True, split, split))
    query_width = w_query.shape[2] // phases
    key_width = w_key.shape[2] // (phases if split else 1)
    first_ring = ring_gather(joined[0], None)
    out_parts = both_layers((w_out[0],), 0, (True,))
    first = section == 0
    other_gain = swapped(norm_gain[0], "section")
    gains = (
        jnp.where(first, norm_gain[0], other_gain),
        jnp.where(first, other_gain, norm_gain[0]),
    )

    matches = destination[:, None] == jnp.arange(replicas, dtype=jnp.int32)[None, :]
    counts = jnp.sum(matches.astype(jnp.int32), axis=0)
    firsts = jnp.min(
        jnp.where(matches, jnp.arange(packed_len, dtype=jnp.int32)[:, None], packed_len), axis=0
    )
    offsets = jnp.arange(capacity, dtype=jnp.int32)
    filled = offsets[None, :] < counts[:, None]
    chosen = jnp.where(filled, firsts[:, None] + offsets[None, :], 0).reshape(-1)
    filled_flat = filled.reshape(-1)
    share = width // (phases * tensors)
    columns = lax.dynamic_slice_in_dim(
        source_tokens, (section * tensors + tensor) * share, share, 1
    )
    send_rows = jnp.where(filled_flat[:, None], columns[chosen], 0).reshape(
        replicas, capacity, share
    )
    send_ids = jnp.where(filled_flat, segment_ids[chosen], -1).reshape(replicas, capacity)
    send_pos = jnp.where(filled_flat, positions[chosen], 0).reshape(replicas, capacity)
    send_rows, _ = lax.optimization_barrier((send_rows, first_ring[0][1]))
    got_rows = lax.all_to_all(send_rows, "dp", split_axis=0, concat_axis=0, tiled=True)
    got_marks = lax.all_to_all(
        jnp.concatenate([send_ids, send_pos], axis=1), "dp", split_axis=0, concat_axis=0, tiled=True
    )
    packed = join(join(got_rows.reshape(packed_len, share), "tensor", 1), "section", 1)
    id_rows = got_marks[:, :capacity].reshape(phases, row_count)
    pos_rows = got_marks[:, capacity:].reshape(phases, row_count)
    factors = turn_factors(pos_rows)
    allowed = (id_rows[:, :, None] == id_rows[:, None, :]) & (
        pos_rows[:, None, :] <= pos_rows[:, :, None]
    )

    starts = [start_of(k) for k in range(replicas)]
    states = [lax.dynamic_slice_in_dim(packed, s, chunk, 1) for s in starts]
    before = None
    for level in range(phases):
        projections, before = ring_gather(joined[level], before) if level else first_ring
        outs, before = ring_gather(out_parts[level], before)
        total = sum(
            jnp.sum(jnp.square(piece.astype(F32)), axis=-1, keepdims=True) for piece in states
        )
        inv_scale = lax.rsqrt(total / width + EPSILON)
        projected = 0.0
        for k in range(replicas):
            gain = lax.dynamic_slice_in_dim(gains[level], starts[k], chunk, 0)
            normed = (states[k].astype(F32) * inv_scale * gain).astype(BF16)
            projected += jnp.dot(normed, projections[k], preferred_element_type=F32)
        mixed_heads = []
        for batch in range(phases):
            part = projected[batch * row_count : (batch + 1) * row_count]
            if batch:
                part, _, _ = lax.optimization_barrier((part, outs[batch], outs[-batch]))
            one = slice(batch, batch + 1)
            mixed_heads.append(
                attend_local(
                    part, allowed[one], [f[one] for f in factors], query_width, key_width
                )
            )
        mixed_heads = jnp.concatenate(mixed_heads, axis=0)
        fresh = [None] * replicas
        half = replicas // 2
        rounds = [[0]] + [[k, replicas - k] for k in range(1, half)] + [[half]]
        for members in rounds:
            terms = jnp.concatenate(
                [jnp.dot(mixed_heads, outs[k], preferred_element_type=F32) for k in members],
                axis=1,
            )
            share_sum = sum_share(sum_share(terms, "section"), "tensor")
            held = jnp.concatenate([states[k] for k in members], axis=1)
            held = lax.dynamic_slice_in_dim(
                held, section * row_count + tensor * row_share, row_share, 0
            )
            result = (held.astype(F32) + share_sum).astype(BF16)
            if level < phases - 1:
                result = join(join(result, "tensor", 0), "section", 0)
            for i, k in enumerate(members):
                fresh[k] = lax.slice_in_dim(result, i * chunk, (i + 1) * chunk, axis=1)
        states = fresh
    final = jnp.zeros((row_share, width), BF16)
    for k in range(replicas):
        final = lax.dynamic_update_slice_in_dim(final, states[k], starts[k], 1)
    return final


def solution(mesh):
    return jax.shard_map(
        per_device,
        mesh=mesh,
        in_specs=(
            P("dp", None),
            P("dp"),
            P("dp"),
            P("dp"),
            P("section", None),
            P("section", "dp", "tensor"),
            P("section", "dp", "tensor"),
            P("section", "dp", "tensor"),
            P("section", "tensor", "dp"),
        ),
        out_specs=P(("dp", "section", "tensor"), None),
        check_vma=False,
    )
```

```python
import jax
import jax.numpy as jnp
from jax import lax
from jax.sharding import PartitionSpec as P

HEAD_DIM = 128


THETA = 500000.0
EPSILON = 1e-05
BF16 = jnp.bfloat16
F32 = jnp.float32


def swapped(array, axis):
    return lax.ppermute(array, axis, [(0, 1), (1, 0)])


def join(array, axis, dim):
    if lax.axis_size(axis) != 2:
        return lax.all_gather(array, axis, axis=dim, tiled=True)
    other = swapped(array, axis)
    first = lax.axis_index(axis) == 0
    return jnp.concatenate(
        [jnp.where(first, array, other), jnp.where(first, other, array)], axis=dim
    )


def sum_share(array, axis):
    if lax.axis_size(axis) != 2:
        return lax.psum_scatter(
            array.astype(BF16), axis, scatter_dimension=0, tiled=True
        ).astype(F32)
    half = array.shape[0] // 2
    first = lax.axis_index(axis) == 0
    mine = jnp.where(first, array[:half], array[half:])
    theirs = jnp.where(first, array[half:], array[:half]).astype(BF16)
    return mine + swapped(theirs, axis).astype(F32)


def both_layers(shards, dim, splits):
    section = lax.axis_index("section")
    mine, give = [], []
    for own, split in zip(shards, splits):
        half = own.shape[dim] // 2
        for place, kept in ((section, mine), (1 - section, give)):
            kept.append(
                lax.dynamic_slice_in_dim(own, place * half, half, dim) if split else own
            )
    mine, give = jnp.concatenate(mine, axis=dim), jnp.concatenate(give, axis=dim)
    got = swapped(give, "section")
    return jnp.where(section == 0, mine, got), jnp.where(section == 0, got, mine)


def ring_order(count):
    return [2 * i for i in range(count // 2)] + [
        2 * i + 1 for i in reversed(range(count // 2))
    ]


def ring_gather(own, before):
    count = lax.axis_size("dp")
    order = ring_order(count)
    right = [(order[i], order[(i + 1) % count]) for i in range(count)]
    left = [(b, a) for a, b in right]
    parts = [None] * count
    parts[0] = own
    onward = back = own
    if before is not None:
        onward, back, _, _ = lax.optimization_barrier((own, own) + before)
    for hop in range(1, count // 2):
        onward = lax.ppermute(onward, "dp", right)
        back = lax.ppermute(back, "dp", left)
        parts[hop], parts[count - hop] = onward, back
    half = own.shape[0] // 2
    top = lax.ppermute(onward[:half], "dp", right)
    low = lax.ppermute(back[half:], "dp", left)
    parts[count // 2] = jnp.concatenate([top, low], axis=0)
    return parts, (onward, back)


def turn_factors(places):
    half_dim = HEAD_DIM // 2
    frequency = THETA ** (-(jnp.arange(half_dim, dtype=F32) * 2.0) / HEAD_DIM)
    angles = places.astype(F32)[..., None] * frequency
    cosine, sine = jnp.cos(angles), jnp.sin(angles)
    return (
        jnp.concatenate([cosine, cosine], axis=-1)[..., None, :],
        jnp.concatenate([sine, sine], axis=-1)[..., None, :],
    )


def rotate(values, factors):
    half_dim = HEAD_DIM // 2
    turned = jnp.concatenate([-values[..., half_dim:], values[..., :half_dim]], axis=-1)
    return values * factors[0] + turned * factors[1]


def attend_local(projected, allowed, factors, query_width, key_width):
    batches, row_len = allowed.shape[:2]
    q_heads = query_width // HEAD_DIM
    kv_heads = key_width // HEAD_DIM
    group_size = q_heads // kv_heads
    projected = projected.reshape(batches, row_len, -1)
    queries = rotate(
        projected[..., :query_width].reshape(batches, row_len, q_heads, HEAD_DIM), factors
    ).astype(BF16)
    queries = queries.reshape(batches, row_len, kv_heads, group_size, HEAD_DIM)
    key_rows = rotate(
        projected[..., query_width : query_width + key_width].reshape(
            batches, row_len, kv_heads, HEAD_DIM
        ),
        factors,
    ).astype(BF16)
    value_rows = (
        projected[..., query_width + key_width :]
        .astype(BF16)
        .reshape(batches, row_len, kv_heads, HEAD_DIM)
    )
    scores = jnp.einsum(
        "brkgd,bskd->bkgrs", queries, key_rows, preferred_element_type=F32
    ) * HEAD_DIM ** (-0.5)
    allowed = allowed[:, None, None]
    scores = jnp.where(allowed, scores, -1e30)
    row_top = jnp.max(scores, axis=-1, keepdims=True)
    powers = jnp.where(allowed, jnp.exp(scores - row_top), 0.0)
    weights = (powers / jnp.sum(powers, axis=-1, keepdims=True)).astype(BF16)
    mixed_heads = jnp.einsum(
        "bkgrs,bskd->brkgd", weights, value_rows, preferred_element_type=F32
    )
    return mixed_heads.astype(BF16).reshape(batches * row_len, query_width)


def per_device(
    source_tokens, destination, segment_ids, positions, norm_gain, w_query, w_key, w_value, w_out
):
    replicas = lax.axis_size("dp")
    phases = lax.axis_size("section")
    tensors = lax.axis_size("tensor")
    section = lax.axis_index("section")
    tensor = lax.axis_index("tensor")
    packed_len, width = source_tokens.shape
    capacity = packed_len // replicas
    row_count = packed_len // phases
    row_share = row_count // tensors
    chunk = width // replicas
    place = lax.axis_index("dp")
    spot = jnp.where(place % 2 == 0, place // 2, replicas - 1 - place // 2)

    def start_of(k):
        there = (spot - k + replicas) % replicas
        owner = jnp.where(there < replicas // 2, 2 * there, 2 * (replicas - 1 - there) + 1)
        return owner * chunk

    split = (w_key.shape[2] // HEAD_DIM) % phases == 0
    joined = both_layers((w_query[0], w_key[0], w_value[0]), 1, (True, split, split))
    query_width = w_query.shape[2] // phases
    key_width = w_key.shape[2] // (phases if split else 1)
    first_ring = ring_gather(joined[0], None)
    out_parts = both_layers((w_out[0],), 0, (True,))
    first = section == 0
    other_gain = swapped(norm_gain[0], "section")
    gains = (
        jnp.where(first, norm_gain[0], other_gain),
        jnp.where(first, other_gain, norm_gain[0]),
    )

    matches = destination[:, None] == jnp.arange(replicas, dtype=jnp.int32)[None, :]
    counts = jnp.sum(matches.astype(jnp.int32), axis=0)
    firsts = jnp.min(
        jnp.where(matches, jnp.arange(packed_len, dtype=jnp.int32)[:, None], packed_len), axis=0
    )
    offsets = jnp.arange(capacity, dtype=jnp.int32)
    filled = offsets[None, :] < counts[:, None]
    chosen = jnp.where(filled, firsts[:, None] + offsets[None, :], 0).reshape(-1)
    filled_flat = filled.reshape(-1)
    share = width // (phases * tensors)
    columns = lax.dynamic_slice_in_dim(
        source_tokens, (section * tensors + tensor) * share, share, 1
    )
    send_rows = jnp.where(filled_flat[:, None], columns[chosen], 0).reshape(
        replicas, capacity, share
    )
    send_ids = jnp.where(filled_flat, segment_ids[chosen], -1).reshape(replicas, capacity)
    send_pos = jnp.where(filled_flat, positions[chosen], 0).reshape(replicas, capacity)
    got_marks = lax.all_to_all(
        jnp.concatenate([send_ids, send_pos], axis=1), "dp", split_axis=0, concat_axis=0, tiled=True
    )
    send_rows, _, got_marks = lax.optimization_barrier((send_rows, first_ring[0][1], got_marks))
    got_rows = lax.all_to_all(send_rows, "dp", split_axis=0, concat_axis=0, tiled=True)
    packed = join(join(got_rows.reshape(packed_len, share), "tensor", 1), "section", 1)
    id_rows = got_marks[:, :capacity].reshape(phases, row_count)
    pos_rows = got_marks[:, capacity:].reshape(phases, row_count)
    factors = turn_factors(pos_rows)
    allowed = (id_rows[:, :, None] == id_rows[:, None, :]) & (
        pos_rows[:, None, :] <= pos_rows[:, :, None]
    )

    starts = [start_of(k) for k in range(replicas)]
    states = [lax.dynamic_slice_in_dim(packed, s, chunk, 1) for s in starts]
    before = None
    for level in range(phases):
        projections, before = ring_gather(joined[level], before) if level else first_ring
        outs, before = ring_gather(out_parts[level], before)
        total = sum(
            jnp.sum(jnp.square(piece.astype(F32)), axis=-1, keepdims=True) for piece in states
        )
        inv_scale = lax.rsqrt(total / width + EPSILON)
        projected = 0.0
        for k in range(replicas):
            gain = lax.dynamic_slice_in_dim(gains[level], starts[k], chunk, 0)
            normed = (states[k].astype(F32) * inv_scale * gain).astype(BF16)
            projected += jnp.dot(normed, projections[k], preferred_element_type=F32)
        mixed_heads = attend_local(projected, allowed, factors, query_width, key_width)
        fresh = [None] * replicas
        half = replicas // 2
        rounds = [[0]] + [[k, replicas - k] for k in range(1, half)] + [[half]]
        for members in rounds:
            terms = jnp.concatenate(
                [jnp.dot(mixed_heads, outs[k], preferred_element_type=F32) for k in members],
                axis=1,
            )
            share_sum = sum_share(sum_share(terms, "section"), "tensor")
            held = jnp.concatenate([states[k] for k in members], axis=1)
            held = lax.dynamic_slice_in_dim(
                held, section * row_count + tensor * row_share, row_share, 0
            )
            result = (held.astype(F32) + share_sum).astype(BF16)
            if level < phases - 1:
                result = join(join(result, "tensor", 0), "section", 0)
            for i, k in enumerate(members):
                fresh[k] = lax.slice_in_dim(result, i * chunk, (i + 1) * chunk, axis=1)
        states = fresh
    final = jnp.zeros((row_share, width), BF16)
    for k in range(replicas):
        final = lax.dynamic_update_slice_in_dim(final, states[k], starts[k], 1)
    return final


def solution(mesh):
    return jax.shard_map(
        per_device,
        mesh=mesh,
        in_specs=(
            P("dp", None),
            P("dp"),
            P("dp"),
            P("dp"),
            P("section", None),
            P("section", "dp", "tensor"),
            P("section", "dp", "tensor"),
            P("section", "dp", "tensor"),
            P("section", "tensor", "dp"),
        ),
        out_specs=P(("dp", "section", "tensor"), None),
        check_vma=False,
    )
```

```python
import jax
import jax.numpy as jnp
from jax import lax
from jax.sharding import PartitionSpec as P

HEAD_DIM = 128


THETA = 500000.0
EPSILON = 1e-05
BF16 = jnp.bfloat16
F32 = jnp.float32


def swapped(array, axis):
    return lax.ppermute(array, axis, [(0, 1), (1, 0)])


def join(array, axis, dim):
    if lax.axis_size(axis) != 2:
        return lax.all_gather(array, axis, axis=dim, tiled=True)
    other = swapped(array, axis)
    first = lax.axis_index(axis) == 0
    return jnp.concatenate(
        [jnp.where(first, array, other), jnp.where(first, other, array)], axis=dim
    )


def sum_share(array, axis):
    if lax.axis_size(axis) != 2:
        return lax.psum_scatter(
            array.astype(BF16), axis, scatter_dimension=0, tiled=True
        ).astype(F32)
    half = array.shape[0] // 2
    first = lax.axis_index(axis) == 0
    mine = jnp.where(first, array[:half], array[half:])
    theirs = jnp.where(first, array[half:], array[:half]).astype(BF16)
    return mine + swapped(theirs, axis).astype(F32)


def both_layers(shards, dim, splits):
    section = lax.axis_index("section")
    mine, give = [], []
    for own, split in zip(shards, splits):
        half = own.shape[dim] // 2
        for place, kept in ((section, mine), (1 - section, give)):
            kept.append(
                lax.dynamic_slice_in_dim(own, place * half, half, dim) if split else own
            )
    mine, give = jnp.concatenate(mine, axis=dim), jnp.concatenate(give, axis=dim)
    got = swapped(give, "section")
    return jnp.where(section == 0, mine, got), jnp.where(section == 0, got, mine)


def ring_order(count):
    return [2 * i for i in range(count // 2)] + [
        2 * i + 1 for i in reversed(range(count // 2))
    ]


def ring_gather(own, before, release):
    count = lax.axis_size("dp")
    order = ring_order(count)
    right = [(order[i], order[(i + 1) % count]) for i in range(count)]
    left = [(b, a) for a, b in right]
    parts = [None] * count
    parts[0] = own
    onward = back = own
    if before is not None:
        onward, back, _, _ = lax.optimization_barrier((own, own) + before)
    for hop in range(1, count // 2):
        onward = lax.ppermute(onward, "dp", right)
        back = lax.ppermute(back, "dp", left)
        parts[hop], parts[count - hop] = onward, back
    half = own.shape[0] // 2
    top = lax.ppermute(onward[:half], "dp", right)
    low = lax.ppermute(back[half:], "dp", left)
    parts[count // 2] = jnp.concatenate([top, low], axis=0)
    return parts, (parts[release], parts[count - release])


def turn_factors(places):
    half_dim = HEAD_DIM // 2
    frequency = THETA ** (-(jnp.arange(half_dim, dtype=F32) * 2.0) / HEAD_DIM)
    angles = places.astype(F32)[..., None] * frequency
    cosine, sine = jnp.cos(angles), jnp.sin(angles)
    return (
        jnp.concatenate([cosine, cosine], axis=-1)[..., None, :],
        jnp.concatenate([sine, sine], axis=-1)[..., None, :],
    )


def rotate(values, factors):
    half_dim = HEAD_DIM // 2
    turned = jnp.concatenate([-values[..., half_dim:], values[..., :half_dim]], axis=-1)
    return values * factors[0] + turned * factors[1]


def attend_local(projected, allowed, factors, query_width, key_width):
    batches, row_len = allowed.shape[:2]
    q_heads = query_width // HEAD_DIM
    kv_heads = key_width // HEAD_DIM
    group_size = q_heads // kv_heads
    projected = projected.reshape(batches, row_len, -1)
    queries = rotate(
        projected[..., :query_width].reshape(batches, row_len, q_heads, HEAD_DIM), factors
    ).astype(BF16)
    queries = queries.reshape(batches, row_len, kv_heads, group_size, HEAD_DIM)
    key_rows = rotate(
        projected[..., query_width : query_width + key_width].reshape(
            batches, row_len, kv_heads, HEAD_DIM
        ),
        factors,
    ).astype(BF16)
    value_rows = (
        projected[..., query_width + key_width :]
        .astype(BF16)
        .reshape(batches, row_len, kv_heads, HEAD_DIM)
    )
    scores = jnp.einsum(
        "brkgd,bskd->bkgrs", queries, key_rows, preferred_element_type=F32
    ) * HEAD_DIM ** (-0.5)
    allowed = allowed[:, None, None]
    scores = jnp.where(allowed, scores, -1e30)
    row_top = jnp.max(scores, axis=-1, keepdims=True)
    powers = jnp.where(allowed, jnp.exp(scores - row_top), 0.0)
    weights = (powers / jnp.sum(powers, axis=-1, keepdims=True)).astype(BF16)
    mixed_heads = jnp.einsum(
        "bkgrs,bskd->brkgd", weights, value_rows, preferred_element_type=F32
    )
    return mixed_heads.astype(BF16).reshape(batches * row_len, query_width)


def per_device(
    source_tokens, destination, segment_ids, positions, norm_gain, w_query, w_key, w_value, w_out
):
    replicas = lax.axis_size("dp")
    phases = lax.axis_size("section")
    tensors = lax.axis_size("tensor")
    section = lax.axis_index("section")
    tensor = lax.axis_index("tensor")
    packed_len, width = source_tokens.shape
    capacity = packed_len // replicas
    row_count = packed_len // phases
    row_share = row_count // tensors
    chunk = width // replicas
    place = lax.axis_index("dp")
    spot = jnp.where(place % 2 == 0, place // 2, replicas - 1 - place // 2)

    def start_of(k):
        there = (spot - k + replicas) % replicas
        owner = jnp.where(there < replicas // 2, 2 * there, 2 * (replicas - 1 - there) + 1)
        return owner * chunk

    split = (w_key.shape[2] // HEAD_DIM) % phases == 0
    joined = both_layers((w_query[0], w_key[0], w_value[0]), 1, (True, split, split))
    query_width = w_query.shape[2] // phases
    key_width = w_key.shape[2] // (phases if split else 1)
    first_ring = ring_gather(joined[0], None, replicas // 2 - 1)
    out_parts = both_layers((w_out[0],), 0, (True,))
    first = section == 0
    other_gain = swapped(norm_gain[0], "section")
    gains = (
        jnp.where(first, norm_gain[0], other_gain),
        jnp.where(first, other_gain, norm_gain[0]),
    )

    matches = destination[:, None] == jnp.arange(replicas, dtype=jnp.int32)[None, :]
    counts = jnp.sum(matches.astype(jnp.int32), axis=0)
    firsts = jnp.min(
        jnp.where(matches, jnp.arange(packed_len, dtype=jnp.int32)[:, None], packed_len), axis=0
    )
    offsets = jnp.arange(capacity, dtype=jnp.int32)
    filled = offsets[None, :] < counts[:, None]
    chosen = jnp.where(filled, firsts[:, None] + offsets[None, :], 0).reshape(-1)
    filled_flat = filled.reshape(-1)
    share = width // (phases * tensors)
    columns = lax.dynamic_slice_in_dim(
        source_tokens, (section * tensors + tensor) * share, share, 1
    )
    send_rows = jnp.where(filled_flat[:, None], columns[chosen], 0).reshape(
        replicas, capacity, share
    )
    send_ids = jnp.where(filled_flat, segment_ids[chosen], -1).reshape(replicas, capacity)
    send_pos = jnp.where(filled_flat, positions[chosen], 0).reshape(replicas, capacity)
    got_marks = lax.all_to_all(
        jnp.concatenate([send_ids, send_pos], axis=1), "dp", split_axis=0, concat_axis=0, tiled=True
    )
    send_rows, _, got_marks = lax.optimization_barrier((send_rows, first_ring[0][1], got_marks))
    got_rows = lax.all_to_all(send_rows, "dp", split_axis=0, concat_axis=0, tiled=True)
    packed = join(join(got_rows.reshape(packed_len, share), "tensor", 1), "section", 1)
    id_rows = got_marks[:, :capacity].reshape(phases, row_count)
    pos_rows = got_marks[:, capacity:].reshape(phases, row_count)
    factors = turn_factors(pos_rows)
    allowed = (id_rows[:, :, None] == id_rows[:, None, :]) & (
        pos_rows[:, None, :] <= pos_rows[:, :, None]
    )

    starts = [start_of(k) for k in range(replicas)]
    states = [lax.dynamic_slice_in_dim(packed, s, chunk, 1) for s in starts]
    before = None
    for level in range(phases):
        projections, before = ring_gather(joined[level], before, replicas // 2 - 2) if level else first_ring
        outs, before = ring_gather(out_parts[level], before, 1)
        total = sum(
            jnp.sum(jnp.square(piece.astype(F32)), axis=-1, keepdims=True) for piece in states
        )
        inv_scale = lax.rsqrt(total / width + EPSILON)
        projected = 0.0
        for k in range(replicas):
            gain = lax.dynamic_slice_in_dim(gains[level], starts[k], chunk, 0)
            normed = (states[k].astype(F32) * inv_scale * gain).astype(BF16)
            projected += jnp.dot(normed, projections[k], preferred_element_type=F32)
        mixed_heads = attend_local(projected, allowed, factors, query_width, key_width)
        fresh = [None] * replicas
        half = replicas // 2
        rounds = [[0]] + [[k, replicas - k] for k in range(1, half)] + [[half]]
        for members in rounds:
            terms = jnp.concatenate(
                [jnp.dot(mixed_heads, outs[k], preferred_element_type=F32) for k in members],
                axis=1,
            )
            share_sum = sum_share(sum_share(terms, "section"), "tensor")
            held = jnp.concatenate([states[k] for k in members], axis=1)
            held = lax.dynamic_slice_in_dim(
                held, section * row_count + tensor * row_share, row_share, 0
            )
            result = (held.astype(F32) + share_sum).astype(BF16)
            if level < phases - 1:
                result = join(join(result, "tensor", 0), "section", 0)
            for i, k in enumerate(members):
                fresh[k] = lax.slice_in_dim(result, i * chunk, (i + 1) * chunk, axis=1)
        states = fresh
    final = jnp.zeros((row_share, width), BF16)
    for k in range(replicas):
        final = lax.dynamic_update_slice_in_dim(final, states[k], starts[k], 1)
    return final


def solution(mesh):
    return jax.shard_map(
        per_device,
        mesh=mesh,
        in_specs=(
            P("dp", None),
            P("dp"),
            P("dp"),
            P("dp"),
            P("section", None),
            P("section", "dp", "tensor"),
            P("section", "dp", "tensor"),
            P("section", "dp", "tensor"),
            P("section", "tensor", "dp"),
        ),
        out_specs=P(("dp", "section", "tensor"), None),
        check_vma=False,
    )
```
